256 devices in a mesh: blk: 4 (over x_hi, core), fsdp: 64 (over y, x_lo, z).
Axes of the slice: x: 4 (x_hi: 2, x_lo: 2; x = x_hi * 2 + x_lo), y: 4, z: 8, core: 2. Of those that a mesh axis runs over, the one named last changes fastest.
Arguments:
- tokens: bfloat16 [4, 24576, 2048], P('blk', 'fsdp'), may hold values from -16 to 16
- cotangent: bfloat16 [4, 24576, 2048], P('blk', 'fsdp'), may hold values from -0.09375 to 0.09375
- segment_ids: int32 [4, 24576], P('blk', 'fsdp'), may hold values from 0 to 767, never falling along the last dimension, each value on 1 to 128 neighbouring positions
- w_qkv: float32 [4, 2048, 1536], P('blk', 'fsdp'), may hold values from -1.06066017 to 1.06066017
- w_out: float32 [4, 1024, 2048], P('blk', 'fsdp'), may hold values from -0.1875 to 0.1875
- m_qkv: float32 [4, 2048, 1536], P('blk', 'fsdp'), may hold values from -4 to 4
- v_qkv: float32 [4, 2048, 1536], P('blk', 'fsdp'), may hold values from 0.05 to 2
- m_out: float32 [4, 1024, 2048], P('blk', 'fsdp'), may hold values from -4 to 4
- v_out: float32 [4, 1024, 2048], P('blk', 'fsdp'), may hold values from 0.05 to 2
Outputs:
- layer_out: bfloat16 [4, 24576, 2048], P('blk', 'fsdp')
- new_qkv: float32 [4, 2048, 1536], P('blk', 'fsdp')
- new_out: float32 [4, 1024, 2048], P('blk', 'fsdp')
- new_m_qkv: float32 [4, 2048, 1536], P('blk', 'fsdp')
- new_v_qkv: float32 [4, 2048, 1536], P('blk', 'fsdp')
- new_m_out: float32 [4, 1024, 2048], P('blk', 'fsdp')
- new_v_out: float32 [4, 1024, 2048], P('blk', 'fsdp')
The draws below stay inside these ranges and needn't reach their ends.
Inputs may be any that keep to these rules, and one draw needn't show every extreme that they name: `segment_ids`: document numbers never fall along a group's tokens; a document holds 1 to 128 tokens.
All inputs are finite; a program needn't handle non-finite values.
Results may differ from the reference program's by a relative error of at most 0.0059.
The reference program's roundings to bfloat16 on the way count: a program that leaves them out, or rounds other values in their place, can miss the bound.
Values may be sent and summed in bfloat16 or wider, within the bound.
No kernel may reach another device: no remote copies, remote signals or barrier semaphores. Data moves between devices by JAX's collectives and lax.ppermute only.
A program may use at most 128 MiB of HBM per device.

```python
import math
import jax
import jax.numpy as jnp
import numpy as np
from jax import lax

D = 2048
HEADS = 8
KV_HEADS = 2
HD = 128
TOK_DEV = 384
HQ = 1024
KVW = 256
COLS = 1536
TOKENS = 24576
N_BLK = 4
N_FSDP = 64


def draw_w_qkv(key, part):
    key = jax.random.fold_in(key, 7)
    base = jnp.clip(jax.random.normal(key, (N_BLK, D, COLS), jnp.float32), -4.0, 4.0) * D ** (-0.5)
    return base


def strengthened(entries, rng, source, target, parts, factor):
    def block_of(dim):
        return (jnp.arange(entries.shape[dim]) // (entries.shape[dim] // parts)).reshape((-1,) + (1,) * (entries.ndim - 1 - dim))

    one_side = jax.random.permutation(rng, parts)[block_of(target)]
    second = (block_of(target) + parts // 2) % parts
    return jnp.where((block_of(source) == one_side) | (block_of(source) == second), factor * entries, entries)


def steps_of(key, extent, split, smallest, top_value):
    factor_of, own = 1.0, jax.random.fold_in(key, 6)
    for dim, blocks in split:
        steps = jnp.exp(jax.random.uniform(jax.random.fold_in(own, dim), (blocks,), jnp.float32, smallest / len(split), top_value / len(split)))
        factor_of = factor_of * jnp.repeat(steps, extent[dim] // blocks).reshape([-1 if axis == dim else 1 for axis in range(len(extent))])
    return factor_of


def split_up(amount, total, most, lean):
    weights = [(1 << 20) // math.isqrt(rank ** lean) + 1 for rank in range(2, amount + 1)]
    rest, counts = total - most - (amount - 1), [1] * (amount - 1)
    while rest > 0:
        candidates = [i for i in range(amount - 1) if counts[i] < most]
        mass, remaining = sum([weights[i] for i in candidates]), rest
        for i in candidates:
            extra = min(most - counts[i], max(1, remaining * weights[i] // mass), rest)
            counts[i] = counts[i] + extra
            rest = rest - extra
    return np.array([most] + counts)


def ragged(own_key, amount, total, reach, skew):
    if amount == 2:
        one = jax.random.randint(own_key, (), max(1, total - reach), min(reach, total - 1) + 1)
        return jnp.stack([one, total - one])
    lengths = jnp.asarray(split_up(amount, total, reach, skew), jnp.int32)
    twos = (amount - 1) // 2
    donor, taker = lengths[1:1 + 2 * twos:2], lengths[2:2 + 2 * twos:2]
    margin = jnp.minimum(donor - 1, reach - taker)
    shifted = jax.random.randint(jax.random.fold_in(own_key, 1), (twos,), 0, 1 << 20) % (margin + 1)
    lengths = lengths.at[1:1 + 2 * twos:2].set(donor - shifted).at[2:2 + 2 * twos:2].set(taker + shifted)
    return lengths[jax.random.permutation(jax.random.fold_in(own_key, 2), amount)]


def bell_draw(stream_key, dims, spread, limit, cuts=(), kind=jnp.bfloat16):
    values = spread * jax.random.normal(stream_key, dims, jnp.float32)
    if cuts:
        values = values * steps_of(stream_key, dims, cuts, -0.22, 0.18)
    return jnp.clip(values, -limit, limit).astype(kind)


def heavy_noise(key, dims, scale, reach, shards, heavy, dtype=jnp.bfloat16):
    values = scale * jax.random.normal(key, dims, jnp.float32)
    if shards:
        values = values * steps_of(key, dims, shards, -0.22, 0.18)
    return jnp.clip(strengthened(values, jax.random.fold_in(key, 3), *heavy), -reach, reach).astype(dtype)


def setup_inputs(seed: int = 0) -> dict:
    keys = jax.random.split(jax.random.key(seed), 10)
    tokens = heavy_noise(keys[0], (N_BLK, TOKENS, D), 1.0, 16.0, ((0, 4), (1, 64)), (1, 2, 64, 4.0))
    cotangent = bell_draw(keys[1], (N_BLK, TOKENS, D), (TOKENS ** -0.5), 0.09375, ((0, 4), (1, 64)))
    segment_ids = jax.vmap(lambda own: jnp.searchsorted(jnp.cumsum(ragged(own, TOKENS // 32, TOKENS, 128, 1)), jnp.arange(TOKENS), side="right"))(jax.random.split(keys[2], N_BLK)).reshape((N_BLK, TOKENS)).astype(jnp.int32)
    w_qkv = draw_w_qkv(jax.random.fold_in(keys[9], 71), 0)
    w_out = bell_draw(keys[4], (N_BLK, HQ, D), HQ ** -0.5, 0.1875, ((0, 4), (1, 64)), jnp.float32)
    m_qkv = bell_draw(keys[5], (N_BLK, D, COLS), 0.5, 4.0, ((0, 4), (1, 64)), jnp.float32)
    v_qkv = jnp.clip(jnp.exp(math.log(2.0) - 3.6888794 * jax.random.uniform(keys[6], (N_BLK, D, COLS), jnp.float32) ** steps_of(keys[6], (N_BLK, D, COLS), ((0, 4), (1, 64)), -0.2, 0.2)), 0.05, 2.0)
    m_out = bell_draw(keys[7], (N_BLK, HQ, D), 0.5, 4.0, ((0, 4), (1, 64)), jnp.float32)
    v_out = jnp.clip(jnp.exp(math.log(2.0) - 3.6888794 * jax.random.uniform(keys[8], (N_BLK, HQ, D), jnp.float32) ** steps_of(keys[8], (N_BLK, HQ, D), ((0, 4), (1, 64)), -0.2, 0.2)), 0.05, 2.0)
    return dict(tokens=tokens, cotangent=cotangent, segment_ids=segment_ids, w_qkv=w_qkv, w_out=w_out, m_qkv=m_qkv, v_qkv=v_qkv, m_out=m_out, v_out=v_out)


norm_eps = 1e-05
beta_one = 0.9
beta_two = 0.95
learn_rate = 0.01
decay_rate = 0.1
adam_eps = 1e-08
masked_score = -1e+30

def float_product(formula, first_op, second_op):
    return jnp.einsum(formula, first_op.astype(jnp.float32), second_op.astype(jnp.float32))

def attend(inputs, segments, full_qkv):
    seq_count, length = (inputs.shape[0], inputs.shape[1])
    group_size = HEADS // KV_HEADS
    widened = inputs.astype(jnp.float32)
    normed = (widened * lax.rsqrt(lax.optimization_barrier(jnp.mean(widened * widened, -1, keepdims=True)) + norm_eps)).astype(jnp.bfloat16)
    joined_rows = float_product('bld,de->ble', normed, full_qkv).astype(jnp.bfloat16)
    queries = joined_rows[..., :HQ].reshape(seq_count, length, KV_HEADS, group_size, HD)
    key_rows = joined_rows[..., HQ:HQ + KVW].reshape(seq_count, length, KV_HEADS, HD)
    value_rows = joined_rows[..., HQ + KVW:].reshape(seq_count, length, KV_HEADS, HD)
    scores = float_product('bqkgd,bskd->bkgqs', queries, key_rows) * HD ** (-0.5)
    position = jnp.arange(length)
    allowed = (segments[:, :, None] == segments[:, None, :]) & (position[:, None] >= position[None, :])
    scores = jnp.where(allowed[:, None, None], scores, masked_score)
    highest = lax.optimization_barrier(jnp.max(scores, -1, keepdims=True))
    raised = jnp.exp(scores - highest)
    attn_probs = raised / lax.optimization_barrier(jnp.sum(raised, -1, keepdims=True))
    probs_low = attn_probs.astype(jnp.bfloat16)
    attended = float_product('bkgqs,bskd->bqkgd', probs_low, value_rows).astype(jnp.bfloat16)
    attended = attended.reshape(seq_count, length, HQ)
    return (normed, queries, key_rows, value_rows, attn_probs, probs_low, attended)

def inner_grads(upstream, queries, key_rows, value_rows, attn_probs, probs_low, full_out):
    seq_count, length = (upstream.shape[0], upstream.shape[1])
    group_size = HEADS // KV_HEADS
    grad_att = float_product('bld,ed->ble', upstream, full_out).astype(jnp.bfloat16)
    grad_att = grad_att.reshape(seq_count, length, KV_HEADS, group_size, HD)
    grad_probs = float_product('bqkgd,bskd->bkgqs', grad_att, value_rows)
    grad_values = float_product('bkgqs,bqkgd->bskd', probs_low, grad_att).astype(jnp.bfloat16)
    centred = grad_probs - lax.optimization_barrier(jnp.sum(grad_probs * attn_probs, -1, keepdims=True))
    grad_scores = (attn_probs * centred * HD ** (-0.5)).astype(jnp.bfloat16)
    grad_queries = float_product('bkgqs,bskd->bqkgd', grad_scores, key_rows).astype(jnp.bfloat16)
    grad_keys = float_product('bkgqs,bqkgd->bskd', grad_scores, queries).astype(jnp.bfloat16)
    return jnp.concatenate([grad_queries.reshape(seq_count, length, HQ), grad_keys.reshape(seq_count, length, KVW), grad_values.reshape(seq_count, length, KVW)], -1)

def adamw(weights, moment, second, gradient, beside):
    moment_new = beta_one * moment + (1.0 - beta_one) * gradient
    second_new = beta_two * second + (1.0 - beta_two) * gradient * gradient
    stepped = weights - learn_rate * (moment_new / (jnp.sqrt(second_new) + adam_eps) + decay_rate * weights)
    return (0.5 * (stepped + beside), moment_new, second_new)

def reference(tokens, cotangent, segment_ids, w_qkv, w_out, m_qkv, v_qkv, m_out, v_out):

    def one_group(group_items):
        inputs, upstream, segments, qkv_master, out_master = group_items
        inputs = inputs.reshape(N_FSDP, TOK_DEV, D)
        upstream = upstream.reshape(N_FSDP, TOK_DEV, D)
        segments = segments.reshape(N_FSDP, TOK_DEV)
        full_qkv = qkv_master.astype(jnp.bfloat16)
        full_out = out_master.astype(jnp.bfloat16)
        normed, queries, key_rows, value_rows, attn_probs, probs_low, attended = attend(inputs, segments, full_qkv)
        layer_out = (inputs.astype(jnp.float32) + float_product('ble,ed->bld', attended, full_out)).astype(jnp.bfloat16)
        grad_out = float_product('ble,bld->ed', attended, upstream)
        joined_grad = inner_grads(upstream, queries, key_rows, value_rows, attn_probs, probs_low, full_out)
        grad_qkv = float_product('bld,ble->de', normed, joined_grad)
        return (layer_out.reshape(TOKENS, D), grad_qkv, grad_out)
    layer_out, grad_qkv, grad_out = lax.map(one_group, (tokens, cotangent, segment_ids, w_qkv, w_out))
    new_qkv, new_m_qkv, new_v_qkv = adamw(w_qkv, m_qkv, v_qkv, grad_qkv, jnp.roll(w_qkv, 1, axis=0))
    new_out, new_m_out, new_v_out = adamw(w_out, m_out, v_out, grad_out, jnp.roll(w_out, 1, axis=0))
    return (layer_out, new_qkv, new_out, new_m_qkv, new_v_qkv, new_m_out, new_v_out)
```

```python
import jax
import jax.numpy as jnp
from jax import lax
from jax.sharding import PartitionSpec as P

HEADS = 8
KV_HEADS = 2
HD = 128
HQ = 1024
KVW = 256
COLS = 1536
RING = 8

norm_eps = 1e-05
beta_one = 0.9
beta_two = 0.95
learn_rate = 0.01
decay_rate = 0.1
adam_eps = 1e-08
masked_score = -1e30

BOTH = ("blk", "fsdp")
F32 = jnp.float32
BF16 = jnp.bfloat16


def coords(device):
    block, index = divmod(device, 64)
    y, x, z = index // 16, index // 8 % 2, index % 8
    cycle = y if x == 0 else 7 - y
    return block, ((z, cycle) if block % 2 == 0 else (cycle, z))


def device_at(block, first, second):
    z, cycle = (first, second) if block % 2 == 0 else (second, first)
    y, x = (cycle, 0) if cycle < 4 else (7 - cycle, 1)
    return block * 64 + y * 16 + x * 8 + z


def ring_shift(value, ring, by):
    pairs = []
    for device in range(256):
        block, (first, second) = coords(device)
        if ring == 0:
            target = device_at(block, (first + by) % RING, second)
        else:
            target = device_at(block, first, (second + by) % RING)
        pairs.append((device, target))
    return lax.ppermute(value, BOTH, pairs)


def absolute_blocks():
    block, index = lax.axis_index("blk"), lax.axis_index("fsdp")
    even = block % 2 == 0
    y, x, z = index // 16, index // 8 % 2, index % 8
    cycle = jnp.where(x == 0, y, 7 - y)
    first, second = jnp.where(even, z, cycle), jnp.where(even, cycle, z)
    steps = jnp.arange(RING)
    first = jnp.broadcast_to(((first + steps) % RING)[None, :], (RING, RING))
    second = jnp.broadcast_to(((second + steps) % RING)[:, None], (RING, RING))
    z, cycle = jnp.where(even, first, second), jnp.where(even, second, first)
    y, x = jnp.where(cycle < 4, cycle, 7 - cycle), (cycle >= 4).astype(jnp.int32)
    return (y * 16 + x * 8 + z).reshape(64)


def reorder_matrix(blocks, rows):
    source = (blocks[:, None] * rows + jnp.arange(rows)[None, :]).reshape(-1)
    return (jnp.arange(64 * rows)[:, None] == source[None, :]).astype(BF16)


def ring_gather(value, ring):
    found = [None] * RING
    found[0] = right = left = value
    for step in range(1, RING // 2):
        right, left = ring_shift(right, ring, 1), ring_shift(left, ring, -1)
        found[RING - step], found[step] = right, left
    half = value.shape[0] // 2
    found[RING // 2] = jnp.concatenate(
        [ring_shift(right[:half], ring, 1), ring_shift(left[half:], ring, -1)], 0
    )
    return found


def ring_scatter(parts, ring):
    half = parts[0].shape[0] // 2
    farthest = parts[RING // 2]
    right = ring_shift(farthest[:half].astype(BF16), ring, 1).astype(F32)
    left = ring_shift(farthest[half:].astype(BF16), ring, -1).astype(F32)
    for step in range(RING // 2 - 1, 0, -1):
        ahead, behind = parts[step], parts[RING - step]
        if step == RING // 2 - 1:
            ahead = jnp.concatenate([ahead[:half] + right, ahead[half:]], 0)
            behind = jnp.concatenate([behind[:half], behind[half:] + left], 0)
        else:
            ahead, behind = ahead + right, behind + left
        right = ring_shift(ahead.astype(BF16), ring, 1).astype(F32)
        left = ring_shift(behind.astype(BF16), ring, -1).astype(F32)
    return parts[0] + right + left


def mixed_product(formula, first_op, second_op):
    return jnp.einsum(formula, first_op, second_op, preferred_element_type=F32)


def attend(joined_rows, segments):
    seq_count, length = joined_rows.shape[:2]
    group_size = HEADS // KV_HEADS
    queries = joined_rows[..., :HQ].reshape(seq_count, length, KV_HEADS, group_size, HD)
    key_rows = joined_rows[..., HQ : HQ + KVW].reshape(seq_count, length, KV_HEADS, HD)
    value_rows = joined_rows[..., HQ + KVW :].reshape(seq_count, length, KV_HEADS, HD)
    scores = mixed_product("bqkgd,bskd->bkgqs", queries, key_rows) * HD ** (-0.5)
    position = jnp.arange(length)
    allowed = (segments[:, :, None] == segments[:, None, :]) & (
        position[:, None] >= position[None, :]
    )
    scores = jnp.where(allowed[:, None, None], scores, masked_score)
    highest = jnp.max(scores, -1, keepdims=True)
    raised = jnp.exp(scores - highest)
    attn_probs = raised / jnp.sum(raised, -1, keepdims=True)
    probs_low = attn_probs.astype(BF16)
    attended = mixed_product("bkgqs,bskd->bqkgd", probs_low, value_rows).astype(BF16)
    attended = attended.reshape(seq_count, length, HQ)
    return (queries, key_rows, value_rows, attn_probs, probs_low, attended)


def inner_grads(grad_att, queries, key_rows, value_rows, attn_probs, probs_low):
    seq_count, length = grad_att.shape[:2]
    group_size = HEADS // KV_HEADS
    grad_att = grad_att.reshape(seq_count, length, KV_HEADS, group_size, HD)
    grad_probs = mixed_product("bqkgd,bskd->bkgqs", grad_att, value_rows)
    grad_values = mixed_product("bkgqs,bqkgd->bskd", probs_low, grad_att).astype(BF16)
    centred = grad_probs - jnp.sum(grad_probs * attn_probs, -1, keepdims=True)
    grad_scores = (attn_probs * centred * HD ** (-0.5)).astype(BF16)
    grad_queries = mixed_product("bkgqs,bskd->bqkgd", grad_scores, key_rows).astype(BF16)
    grad_keys = mixed_product("bkgqs,bqkgd->bskd", grad_scores, queries).astype(BF16)
    return jnp.concatenate(
        [
            grad_queries.reshape(seq_count, length, HQ),
            grad_keys.reshape(seq_count, length, KVW),
            grad_values.reshape(seq_count, length, KVW),
        ],
        -1,
    )


def adamw(weights, moment, second, gradient, beside):
    moment_new = beta_one * moment + (1.0 - beta_one) * gradient
    second_new = beta_two * second + (1.0 - beta_two) * gradient * gradient
    stepped = weights - learn_rate * (
        moment_new / (jnp.sqrt(second_new) + adam_eps) + decay_rate * weights
    )
    return (0.5 * (stepped + beside), moment_new, second_new)


def to_rows(out_rows):
    split = out_rows.reshape(-1, 16, 2, 1024)
    return split.transpose(0, 2, 1, 3).reshape(-1, 1024)


def from_rows(rows):
    split = rows.reshape(-1, 2, 16, 1024)
    return split.transpose(0, 2, 1, 3).reshape(-1, 2048)


def per_device(tokens, cotangent, segment_ids, w_qkv, w_out, m_qkv, v_qkv, m_out, v_out):
    own = jnp.concatenate([w_qkv[0].astype(BF16), to_rows(w_out[0].astype(BF16))], 1)
    line = jnp.concatenate(ring_gather(own, 0), 0)
    gathered = ring_gather(line, 1)
    full_qkv = jnp.concatenate([part[:, :COLS] for part in gathered], 0)
    full_out = jnp.concatenate([from_rows(part[:, COLS:]) for part in gathered], 0)

    beside = lax.ppermute(own, "blk", [(i, (i + 1) % 4) for i in range(4)]).astype(F32)
    beside_qkv, beside_out = beside[:, :COLS][None], from_rows(beside[:, COLS:])[None]

    blocks = absolute_blocks()
    reorder_in = reorder_matrix(blocks, 32)
    reorder_heads = reorder_matrix(blocks, 16)

    widened = tokens.astype(F32)
    normed = (
        widened * lax.rsqrt(jnp.mean(widened * widened, -1, keepdims=True) + norm_eps)
    ).astype(BF16)
    normed = mixed_product("bld,de->ble", normed, reorder_in).astype(BF16)

    joined_rows = mixed_product("bld,de->ble", normed, full_qkv).astype(BF16)
    queries, key_rows, value_rows, attn_probs, probs_low, attended = attend(
        joined_rows, segment_ids
    )
    attended = mixed_product("ble,ef->blf", attended, reorder_heads).astype(BF16)
    layer_out = (
        tokens.astype(F32) + mixed_product("ble,ed->bld", attended, full_out)
    ).astype(BF16)
    grad_out_full = mixed_product("ble,bld->ed", attended, cotangent)
    grad_att = mixed_product("bld,ed->ble", cotangent, full_out).astype(BF16)
    grad_att = mixed_product("blf,ef->ble", grad_att, reorder_heads).astype(BF16)
    joined_grad = inner_grads(
        grad_att, queries, key_rows, value_rows, attn_probs, probs_low
    )
    grad_qkv_full = mixed_product("bld,ble->de", normed, joined_grad)

    shares = [
        jnp.concatenate(
            [
                grad_qkv_full[256 * k : 256 * (k + 1)],
                to_rows(grad_out_full[128 * k : 128 * (k + 1)]),
            ],
            1,
        )
        for k in range(RING)
    ]
    line_sum = ring_scatter(shares, 1)
    summed = ring_scatter([line_sum[32 * k : 32 * (k + 1)] for k in range(RING)], 0)
    grad_qkv, grad_out = summed[:, :COLS], from_rows(summed[:, COLS:])

    new_qkv, new_m_qkv, new_v_qkv = adamw(w_qkv, m_qkv, v_qkv, grad_qkv[None], beside_qkv)
    new_out, new_m_out, new_v_out = adamw(w_out, m_out, v_out, grad_out[None], beside_out)
    return (layer_out, new_qkv, new_out, new_m_qkv, new_v_qkv, new_m_out, new_v_out)


def solution(mesh):
    rows, row = P("blk", "fsdp", None), P("blk", "fsdp")
    return jax.shard_map(
        per_device,
        mesh=mesh,
        in_specs=(rows, rows, row) + (rows,) * 6,
        out_specs=(rows,) * 7,
        check_vma=False,
    )
```

```python
import functools

import jax
import jax.numpy as jnp
from jax import lax
from jax.experimental import pallas as pl
from jax.experimental.pallas import tpu as pltpu
from jax.sharding import PartitionSpec as P

HEADS = 8
KV_HEADS = 2
HD = 128
HQ = 1024
KVW = 256
COLS = 1536
RING = 8
LENGTH = 384
BLOCK = 128
GROUP = HEADS // KV_HEADS

norm_eps = 1e-05
beta_one = 0.9
beta_two = 0.95
learn_rate = 0.01
decay_rate = 0.1
adam_eps = 1e-08
masked_score = -1e30

BOTH = ("blk", "fsdp")
F32 = jnp.float32
BF16 = jnp.bfloat16


def coords(device):
    block, index = divmod(device, 64)
    y, x, z = index // 16, index // 8 % 2, index % 8
    cycle = y if x == 0 else 7 - y
    return block, ((z, cycle) if block % 2 == 0 else (cycle, z))


def device_at(block, first, second):
    z, cycle = (first, second) if block % 2 == 0 else (second, first)
    y, x = (cycle, 0) if cycle < 4 else (7 - cycle, 1)
    return block * 64 + y * 16 + x * 8 + z


def ring_shift(value, ring, by):
    pairs = []
    for device in range(256):
        block, (first, second) = coords(device)
        if ring == 0:
            target = device_at(block, (first + by) % RING, second)
        else:
            target = device_at(block, first, (second + by) % RING)
        pairs.append((device, target))
    return lax.ppermute(value, BOTH, pairs)


def absolute_blocks():
    block, index = lax.axis_index("blk"), lax.axis_index("fsdp")
    even = block % 2 == 0
    y, x, z = index // 16, index // 8 % 2, index % 8
    cycle = jnp.where(x == 0, y, 7 - y)
    first, second = jnp.where(even, z, cycle), jnp.where(even, cycle, z)
    steps = jnp.arange(RING)
    first = jnp.broadcast_to(((first + steps) % RING)[None, :], (RING, RING))
    second = jnp.broadcast_to(((second + steps) % RING)[:, None], (RING, RING))
    z, cycle = jnp.where(even, first, second), jnp.where(even, second, first)
    y, x = jnp.where(cycle < 4, cycle, 7 - cycle), (cycle >= 4).astype(jnp.int32)
    return (y * 16 + x * 8 + z).reshape(64)


def reorder_matrix(blocks, rows):
    source = (blocks[:, None] * rows + jnp.arange(rows)[None, :]).reshape(-1)
    return (jnp.arange(64 * rows)[:, None] == source[None, :]).astype(BF16)


def shifts(pair, ring, places=1):
    return ring_shift(pair[0], ring, places), ring_shift(pair[1], ring, -places)


def halves(pair):
    half = pair[0].shape[0] // 2
    return pair[0][:half], pair[1][half:]


def tie(*trees):
    return lax.optimization_barrier(trees)


def by_offset(own, steps):
    one, two, three, four = steps
    return [own, one[1], two[1], three[1], jnp.concatenate(four, 0), three[0], two[0], one[0]]


def low(pair):
    return pair[0].astype(BF16), pair[1].astype(BF16)


def add_on(shares, pair):
    return shares[0] + pair[0].astype(F32), shares[1] + pair[1].astype(F32)


def add_halves(shares, pair):
    half = shares[0].shape[0] // 2
    up, down = pair[0].astype(F32), pair[1].astype(F32)
    return (
        jnp.concatenate([shares[0][:half] + up, shares[0][half:]], 0),
        jnp.concatenate([shares[1][:half], shares[1][half:] + down], 0),
    )


def mixed_product(formula, first_op, second_op):
    return jnp.einsum(formula, first_op, second_op, preferred_element_type=F32)


def block_probs(joined, seg_col, seg_row, kv, block):
    low, high = block * BLOCK, (block + 1) * BLOCK
    start = max(low - BLOCK, 0)
    queries = jnp.concatenate(
        [joined[low:high, HD * head : HD * (head + 1)] for head in range(GROUP * kv, GROUP * (kv + 1))], 0
    )
    keys = joined[start:high, HQ + HD * kv : HQ + HD * (kv + 1)]
    scores = lax.dot_general(
        queries, keys, (((1,), (1,)), ((), ())), preferred_element_type=F32
    ) * HD ** (-0.5)
    shape = (BLOCK, high - start)
    position = low + lax.broadcasted_iota(jnp.int32, shape, 0)
    other = start + lax.broadcasted_iota(jnp.int32, shape, 1)
    allowed = (seg_col[low:high, :] == seg_row[:, start:high]) & (position >= other)
    bias = jnp.where(allowed, 1, 0)
    scores = jnp.where(jnp.concatenate([bias] * GROUP, 0) > 0, scores, masked_score)
    raised = jnp.exp(scores - jnp.max(scores, -1, keepdims=True))
    return queries, keys, raised / jnp.sum(raised, -1, keepdims=True)


def forward_kernel(joined, seg_col, seg_row, reorder, attended, plain):
    for kv in range(KV_HEADS):
        for block in range(3):
            low, high = block * BLOCK, (block + 1) * BLOCK
            start = max(low - BLOCK, 0)
            _, _, probs = block_probs(joined, seg_col, seg_row, kv, block)
            values = joined[start:high, HQ + KVW + HD * kv : HQ + KVW + HD * (kv + 1)]
            found = jnp.dot(probs.astype(BF16), values, preferred_element_type=F32).astype(BF16)
            for head in range(GROUP):
                at = HD * (GROUP * kv + head)
                plain[low:high, at : at + HD] = found[BLOCK * head : BLOCK * (head + 1)]
    attended[...] = jnp.dot(plain[...], reorder[...], preferred_element_type=F32).astype(BF16)


def backward_kernel(kv, joined, seg_col, seg_row, reorder, grad_rel, grads, upstream, kv_sums):
    wide = GROUP * HD
    upstream[...] = lax.dot_general(
        grad_rel[...], reorder[wide * kv : wide * (kv + 1)], (((1,), (1,)), ((), ())), preferred_element_type=F32
    ).astype(BF16)
    across = (((0,), (0,)), ((), ()))
    kv_sums[...] = jnp.zeros_like(kv_sums)
    for block in range(3):
        low, high = block * BLOCK, (block + 1) * BLOCK
        start = max(low - BLOCK, 0)
        queries, keys, probs = block_probs(joined, seg_col, seg_row, kv, block)
        values = joined[start:high, HQ + KVW + HD * kv : HQ + KVW + HD * (kv + 1)]
        grad_att = jnp.concatenate(
            [upstream[low:high, HD * head : HD * (head + 1)] for head in range(GROUP)], 0
        )
        grad_probs = lax.dot_general(
            grad_att, values, (((1,), (1,)), ((), ())), preferred_element_type=F32
        )
        kv_sums[start:high, HD:] += lax.dot_general(
            probs.astype(BF16), grad_att, across, preferred_element_type=F32
        )
        centred = grad_probs - jnp.sum(grad_probs * probs, -1, keepdims=True)
        grad_scores = (probs * centred * HD ** (-0.5)).astype(BF16)
        found = jnp.dot(grad_scores, keys, preferred_element_type=F32).astype(BF16)
        for head in range(GROUP):
            grads[low:high, HD * head : HD * (head + 1)] = found[BLOCK * head : BLOCK * (head + 1)]
        kv_sums[start:high, :HD] += lax.dot_general(
            grad_scores, queries, across, preferred_element_type=F32
        )
    grads[:, wide:] = kv_sums[...].astype(BF16)


def on_core(kernel, width, scratch, flops, *operands):
    whole = pl.BlockSpec(memory_space=pltpu.VMEM)
    return pl.pallas_call(
        kernel,
        out_shape=jax.ShapeDtypeStruct((LENGTH, width), BF16),
        in_specs=[whole] * len(operands),
        out_specs=whole,
        scratch_shapes=scratch,
        compiler_params=pltpu.CompilerParams(vmem_limit_bytes=40 * 2**20),
        cost_estimate=pl.CostEstimate(flops=flops, bytes_accessed=6 * 2**20, transcendentals=2**20),
    )(*operands)


def adamw(weights, moment, second, gradient, beside):
    moment_new = beta_one * moment + (1.0 - beta_one) * gradient
    second_new = beta_two * second + (1.0 - beta_two) * gradient * gradient
    stepped = weights - learn_rate * (
        moment_new / (jnp.sqrt(second_new) + adam_eps) + decay_rate * weights
    )
    return (0.5 * (stepped + beside), moment_new, second_new)


def to_rows(out_rows):
    left = out_rows[:, :1024].reshape(-1, 16, 1024)
    right = out_rows[:, 1024:].reshape(-1, 16, 1024)
    return jnp.concatenate([left, right], 1).reshape(-1, 1024)


def from_rows(rows):
    split = rows.reshape(-1, 32, 1024)
    left, right = split[:, :16].reshape(-1, 1024), split[:, 16:].reshape(-1, 1024)
    return jnp.concatenate([left, right], 1)


def sort_kernel(*refs):
    *pieces, rows_qkv, rows_out = refs
    at = 0
    for piece in pieces:
        rows = piece.shape[0]
        rows_qkv[at : at + rows] = piece[:, :COLS]
        half = at % 32 // 16
        for part in range(rows // 16):
            low, side = at // 32 * 16, 1024 * (half + part)
            rows_out[low : low + 16, side : side + 1024] = piece[16 * part : 16 * (part + 1), COLS:]
        at += rows


def sort_pieces(*pieces):
    whole = pl.BlockSpec(memory_space=pltpu.VMEM)
    return pl.pallas_call(
        sort_kernel,
        out_shape=(
            jax.ShapeDtypeStruct((256, COLS), BF16),
            jax.ShapeDtypeStruct((128, 2048), BF16),
        ),
        in_specs=[whole] * len(pieces),
        out_specs=(whole, whole),
        compiler_params=pltpu.CompilerParams(vmem_limit_bytes=16 * 2**20),
    )(*pieces)


def gather_rows(own, prepare):
    s1 = shifts((own, own), 0)
    s2 = shifts(s1, 0)
    s3 = shifts(s2, 0)
    s4 = shifts(halves(s3), 0)
    line_qkv, line_out = sort_pieces(
        own, s1[1], s2[1], s3[1], s4[0], s4[1], s3[0], s2[0], s1[0]
    )
    line_qkv, line_out, blocks, own = tie(line_qkv, line_out, absolute_blocks(), own)
    prepared = prepare(blocks)
    q1 = shifts((line_qkv, line_qkv), 1)
    q1, line_out, prepared = tie(q1, line_out, prepared)
    q2 = shifts(q1, 1)
    o1 = shifts((line_out, line_out), 1)
    q3 = shifts(q2, 1)
    o2 = shifts(o1, 1)
    q4 = shifts(halves(q3), 1)
    o3 = shifts(o2, 1)
    o4 = shifts(halves(o3), 1)
    return (line_qkv, q1, q2, q3, q4), (line_out, o1, o2, o3, o4), own, prepared


def line_sum(share, waiting, after_first=None):
    farthest = share(4, waiting)
    half = farthest.shape[0] // 2
    beside = share(3, waiting), share(5, waiting)
    moved = shifts(low((farthest[:half], farthest[half:])), 1)
    moved, waiting, after_first = tie(moved, waiting, after_first)
    sums = add_halves(beside, moved)
    for step in (2, 1):
        beside = share(step, waiting), share(RING - step, waiting)
        moved = shifts(low(sums), 1)
        moved, waiting = tie(moved, waiting)
        sums = add_on(beside, moved)
    last = share(0, waiting)
    moved = shifts(low(sums), 1)
    return last + moved[0].astype(F32) + moved[1].astype(F32), after_first


def small_sum(rows):
    place = lambda k: rows[32 * k : 32 * (k + 1)]
    farthest = shifts(low((place(4)[:16], place(4)[16:])), 0, 2)
    far = shifts(low((place(3), place(5))), 0)
    sums = add_halves(add_on((place(2), place(6)), far), farthest)
    near = shifts(low((place(1), place(7))), 0)
    middle = shifts(low(sums), 0, 2)
    return place(0) + sum(part.astype(F32) for part in near + middle)


def per_device(tokens, cotangent, segment_ids, w_qkv, w_out, m_qkv, v_qkv, m_out, v_out):
    own = jnp.concatenate([w_qkv[0].astype(BF16), to_rows(w_out[0].astype(BF16))], 1)
    widened = tokens[0].astype(F32)
    normed = (
        widened * lax.rsqrt(jnp.mean(widened * widened, -1, keepdims=True) + norm_eps)
    ).astype(BF16)

    def prepare(blocks):
        return (
            mixed_product("ld,de->le", normed, reorder_matrix(blocks, 32)).astype(BF16),
            reorder_matrix(blocks, 16),
        )

    (line_qkv, q1, q2, q3, q4), (line_out, *moved_out), own_late, (normed, reorder_heads) = gather_rows(
        own, prepare
    )
    beside = lax.ppermute(own_late, "blk", [(i, (i + 1) % 4) for i in range(4)]).astype(F32)
    beside_qkv, beside_out = beside[:, :COLS][None], from_rows(beside[:, COLS:])[None]

    seg_row = segment_ids
    seg_col = segment_ids.reshape(LENGTH, 1)

    joined = 0.0
    for low_row, part in (
        (0, line_qkv), (256, q1[1]), (1792, q1[0]), (512, q2[1]), (1536, q2[0]),
        (768, q3[1]), (1280, q3[0]), (1024, q4[0]), (1152, q4[1]),
    ):
        features = normed[:, low_row : low_row + part.shape[0]]
        joined = joined + mixed_product("ld,de->le", features, part)
    joined = joined.astype(BF16)
    attended = on_core(
        forward_kernel, HQ, [pltpu.VMEM((LENGTH, HQ), BF16)], 1300000000,
        joined, seg_col, seg_row, reorder_heads,
    )
    moved_out, attended = tie(moved_out, attended)
    full_out = jnp.concatenate(by_offset(line_out, moved_out), 0)
    sum_out, joined_late = line_sum(
        lambda k, held: mixed_product("ld,le->de", held[:, 128 * k : 128 * (k + 1)], cotangent[0]),
        attended, joined,
    )
    grad_rel = mixed_product("ld,ed->le", cotangent[0], full_out).astype(BF16)
    grads = [
        on_core(
            functools.partial(backward_kernel, kv), (GROUP + 2) * HD,
            [pltpu.VMEM((LENGTH, GROUP * HD), BF16), pltpu.VMEM((LENGTH, 2 * HD), F32)], 1250000000,
            source, seg_col, seg_row, reorder_heads, grad_rel,
        )
        for kv, source in enumerate((joined, joined_late))
    ]
    wide = GROUP * HD
    joined_grad = jnp.concatenate(
        [
            *[part[:, :wide] for part in grads],
            *[part[:, wide : wide + HD] for part in grads],
            *[part[:, wide + HD :] for part in grads],
        ],
        1,
    )
    sum_qkv, _ = line_sum(
        lambda k, held: mixed_product("ld,le->de", normed[:, 256 * k : 256 * (k + 1)], held), joined_grad
    )
    layer_out = (
        tokens[0].astype(F32) + mixed_product("le,ed->ld", attended, full_out)
    ).astype(BF16)
    summed = small_sum(jnp.concatenate([sum_qkv, to_rows(sum_out)], 1))
    grad_qkv, grad_out = summed[:, :COLS], from_rows(summed[:, COLS:])

    new_qkv, new_m_qkv, new_v_qkv = adamw(w_qkv, m_qkv, v_qkv, grad_qkv[None], beside_qkv)
    new_out, new_m_out, new_v_out = adamw(w_out, m_out, v_out, grad_out[None], beside_out)
    return (layer_out[None], new_qkv, new_out, new_m_qkv, new_v_qkv, new_m_out, new_v_out)


def solution(mesh):
    rows, row = P("blk", "fsdp", None), P("blk", "fsdp")
    return jax.shard_map(
        per_device,
        mesh=mesh,
        in_specs=(rows, rows, row) + (rows,) * 6,
        out_specs=(rows,) * 7,
        check_vma=False,
    )
```

```python
import functools

import jax
import jax.numpy as jnp
from jax import lax
from jax.experimental import pallas as pl
from jax.experimental.pallas import tpu as pltpu
from jax.sharding import PartitionSpec as P

HEADS = 8
KV_HEADS = 2
HD = 128
HQ = 1024
KVW = 256
COLS = 1536
RING = 8
LENGTH = 384
BLOCK = 128
GROUP = HEADS // KV_HEADS

norm_eps = 1e-05
beta_one = 0.9
beta_two = 0.95
learn_rate = 0.01
decay_rate = 0.1
adam_eps = 1e-08
masked_score = -1e30

BOTH = ("blk", "fsdp")
F32 = jnp.float32
BF16 = jnp.bfloat16


def coords(device):
    block, index = divmod(device, 64)
    y, x, z = index // 16, index // 8 % 2, index % 8
    cycle = y if x == 0 else 7 - y
    return block, ((z, cycle) if block % 2 == 0 else (cycle, z))


def device_at(block, first, second):
    z, cycle = (first, second) if block % 2 == 0 else (second, first)
    y, x = (cycle, 0) if cycle < 4 else (7 - cycle, 1)
    return block * 64 + y * 16 + x * 8 + z


def ring_shift(value, ring, by):
    pairs = []
    for device in range(256):
        block, (first, second) = coords(device)
        if ring == 0:
            target = device_at(block, (first + by) % RING, second)
        else:
            target = device_at(block, first, (second + by) % RING)
        pairs.append((device, target))
    return lax.ppermute(value, BOTH, pairs)


def absolute_blocks():
    block, index = lax.axis_index("blk"), lax.axis_index("fsdp")
    even = block % 2 == 0
    y, x, z = index // 16, index // 8 % 2, index % 8
    cycle = jnp.where(x == 0, y, 7 - y)
    first, second = jnp.where(even, z, cycle), jnp.where(even, cycle, z)
    steps = jnp.arange(RING)
    first = jnp.broadcast_to(((first + steps) % RING)[None, :], (RING, RING))
    second = jnp.broadcast_to(((second + steps) % RING)[:, None], (RING, RING))
    z, cycle = jnp.where(even, first, second), jnp.where(even, second, first)
    y, x = jnp.where(cycle < 4, cycle, 7 - cycle), (cycle >= 4).astype(jnp.int32)
    return (y * 16 + x * 8 + z).reshape(64)


def reorder_matrix(blocks, rows):
    source = (blocks[:, None] * rows + jnp.arange(rows)[None, :]).reshape(-1)
    return (jnp.arange(64 * rows)[:, None] == source[None, :]).astype(BF16)


def shifts(pair, ring, places=1):
    return ring_shift(pair[0], ring, places), ring_shift(pair[1], ring, -places)


def halves(pair):
    half = pair[0].shape[0] // 2
    return pair[0][:half], pair[1][half:]


def tie(*trees):
    return lax.optimization_barrier(trees)


def by_offset(own, steps):
    one, two, three, four = steps
    return [own, one[1], two[1], three[1], jnp.concatenate(four, 0), three[0], two[0], one[0]]


def low(pair):
    return pair[0].astype(BF16), pair[1].astype(BF16)


def add_on(shares, pair):
    return shares[0] + pair[0].astype(F32), shares[1] + pair[1].astype(F32)


def add_halves(shares, pair):
    half = shares[0].shape[0] // 2
    up, down = pair[0].astype(F32), pair[1].astype(F32)
    return (
        jnp.concatenate([shares[0][:half] + up, shares[0][half:]], 0),
        jnp.concatenate([shares[1][:half], shares[1][half:] + down], 0),
    )


def mixed_product(formula, first_op, second_op):
    return jnp.einsum(formula, first_op, second_op, preferred_element_type=F32)


def block_probs(joined, seg_col, seg_row, kv, block):
    low, high = block * BLOCK, (block + 1) * BLOCK
    start = max(low - BLOCK, 0)
    queries = jnp.concatenate(
        [joined[low:high, HD * head : HD * (head + 1)] for head in range(GROUP * kv, GROUP * (kv + 1))], 0
    )
    keys = joined[start:high, HQ + HD * kv : HQ + HD * (kv + 1)]
    scores = lax.dot_general(
        queries, keys, (((1,), (1,)), ((), ())), preferred_element_type=F32
    ) * HD ** (-0.5)
    shape = (BLOCK, high - start)
    position = low + lax.broadcasted_iota(jnp.int32, shape, 0)
    other = start + lax.broadcasted_iota(jnp.int32, shape, 1)
    allowed = (seg_col[low:high, :] == seg_row[:, start:high]) & (position >= other)
    bias = jnp.where(allowed, 1, 0)
    scores = jnp.where(jnp.concatenate([bias] * GROUP, 0) > 0, scores, masked_score)
    raised = jnp.exp(scores - jnp.max(scores, -1, keepdims=True))
    return queries, keys, raised / jnp.sum(raised, -1, keepdims=True)


def forward_kernel(joined, seg_col, seg_row, reorder, attended, plain):
    for kv in range(KV_HEADS):
        for block in range(3):
            low, high = block * BLOCK, (block + 1) * BLOCK
            start = max(low - BLOCK, 0)
            _, _, probs = block_probs(joined, seg_col, seg_row, kv, block)
            values = joined[start:high, HQ + KVW + HD * kv : HQ + KVW + HD * (kv + 1)]
            found = jnp.dot(probs.astype(BF16), values, preferred_element_type=F32).astype(BF16)
            for head in range(GROUP):
                at = HD * (GROUP * kv + head)
                plain[low:high, at : at + HD] = found[BLOCK * head : BLOCK * (head + 1)]
    attended[...] = jnp.dot(plain[...], reorder[...], preferred_element_type=F32).astype(BF16)


def backward_kernel(kv, joined, seg_col, seg_row, reorder, grad_rel, grads, upstream, kv_sums):
    wide = GROUP * HD
    upstream[...] = lax.dot_general(
        grad_rel[...], reorder[wide * kv : wide * (kv + 1)], (((1,), (1,)), ((), ())), preferred_element_type=F32
    ).astype(BF16)
    across = (((0,), (0,)), ((), ()))
    kv_sums[...] = jnp.zeros_like(kv_sums)
    for block in range(3):
        low, high = block * BLOCK, (block + 1) * BLOCK
        start = max(low - BLOCK, 0)
        queries, keys, probs = block_probs(joined, seg_col, seg_row, kv, block)
        values = joined[start:high, HQ + KVW + HD * kv : HQ + KVW + HD * (kv + 1)]
        grad_att = jnp.concatenate(
            [upstream[low:high, HD * head : HD * (head + 1)] for head in range(GROUP)], 0
        )
        grad_probs = lax.dot_general(
            grad_att, values, (((1,), (1,)), ((), ())), preferred_element_type=F32
        )
        kv_sums[start:high, HD:] += lax.dot_general(
            probs.astype(BF16), grad_att, across, preferred_element_type=F32
        )
        centred = grad_probs - jnp.sum(grad_probs * probs, -1, keepdims=True)
        grad_scores = (probs * centred * HD ** (-0.5)).astype(BF16)
        found = jnp.dot(grad_scores, keys, preferred_element_type=F32).astype(BF16)
        for head in range(GROUP):
            grads[low:high, HD * head : HD * (head + 1)] = found[BLOCK * head : BLOCK * (head + 1)]
        kv_sums[start:high, :HD] += lax.dot_general(
            grad_scores, queries, across, preferred_element_type=F32
        )
    grads[:, wide:] = kv_sums[...].astype(BF16)


def on_core(kernel, width, scratch, flops, *operands):
    whole = pl.BlockSpec(memory_space=pltpu.VMEM)
    return pl.pallas_call(
        kernel,
        out_shape=jax.ShapeDtypeStruct((LENGTH, width), BF16),
        in_specs=[whole] * len(operands),
        out_specs=whole,
        scratch_shapes=scratch,
        compiler_params=pltpu.CompilerParams(vmem_limit_bytes=40 * 2**20),
        cost_estimate=pl.CostEstimate(flops=flops, bytes_accessed=6 * 2**20, transcendentals=2**20),
    )(*operands)


def adamw(weights, moment, second, gradient, beside):
    moment_new = beta_one * moment + (1.0 - beta_one) * gradient
    second_new = beta_two * second + (1.0 - beta_two) * gradient * gradient
    stepped = weights - learn_rate * (
        moment_new / (jnp.sqrt(second_new) + adam_eps) + decay_rate * weights
    )
    return (0.5 * (stepped + beside), moment_new, second_new)


def to_rows(out_rows):
    left = out_rows[:, :1024].reshape(-1, 16, 1024)
    right = out_rows[:, 1024:].reshape(-1, 16, 1024)
    return jnp.concatenate([left, right], 1).reshape(-1, 1024)


def from_rows(rows):
    split = rows.reshape(-1, 32, 1024)
    left, right = split[:, :16].reshape(-1, 1024), split[:, 16:].reshape(-1, 1024)
    return jnp.concatenate([left, right], 1)


def sort_kernel(*refs):
    *pieces, rows_qkv, rows_out = refs
    at = 0
    for piece in pieces:
        rows = piece.shape[0]
        rows_qkv[at : at + rows] = piece[:, :COLS]
        half = at % 32 // 16
        for part in range(rows // 16):
            low, side = at // 32 * 16, 1024 * (half + part)
            rows_out[low : low + 16, side : side + 1024] = piece[16 * part : 16 * (part + 1), COLS:]
        at += rows


def sort_pieces(*pieces):
    whole = pl.BlockSpec(memory_space=pltpu.VMEM)
    return pl.pallas_call(
        sort_kernel,
        out_shape=(
            jax.ShapeDtypeStruct((256, COLS), BF16),
            jax.ShapeDtypeStruct((128, 2048), BF16),
        ),
        in_specs=[whole] * len(pieces),
        out_specs=(whole, whole),
        compiler_params=pltpu.CompilerParams(vmem_limit_bytes=16 * 2**20),
    )(*pieces)


def gather_rows(own, prepare):
    s1 = shifts((own, own), 0)
    s2 = shifts(s1, 0)
    s3 = shifts(s2, 0)
    s4 = shifts(halves(s3), 0)
    line_qkv, line_out = sort_pieces(
        own, s1[1], s2[1], s3[1], s4[0], s4[1], s3[0], s2[0], s1[0]
    )
    line_qkv, line_out, blocks = tie(line_qkv, line_out, absolute_blocks())
    prepared = prepare(blocks)
    q1 = shifts((line_qkv, line_qkv), 1)
    q1, line_out, prepared = tie(q1, line_out, prepared)
    q2 = shifts(q1, 1)
    o1 = shifts((line_out, line_out), 1)
    q3 = shifts(q2, 1)
    o2 = shifts(o1, 1)
    q3, own = tie(q3, own)
    q4 = shifts(halves(q3), 1)
    o3 = shifts(o2, 1)
    o4 = shifts(halves(o3), 1)
    return (line_qkv, q1, q2, q3, q4), (line_out, o1, o2, o3, o4), own, prepared


def line_sum(share, waiting, after_first=None):
    farthest = share(4, waiting)
    half = farthest.shape[0] // 2
    beside = share(3, waiting), share(5, waiting)
    moved = shifts(low((farthest[:half], farthest[half:])), 1)
    moved, waiting, after_first = tie(moved, waiting, after_first)
    sums = add_halves(beside, moved)
    for step in (2, 1):
        beside = share(step, waiting), share(RING - step, waiting)
        moved = shifts(low(sums), 1)
        moved, waiting = tie(moved, waiting)
        sums = add_on(beside, moved)
    last = share(0, waiting)
    moved = shifts(low(sums), 1)
    return last + moved[0].astype(F32) + moved[1].astype(F32), after_first


def small_sum(rows):
    place = lambda k: rows[32 * k : 32 * (k + 1)]
    farthest = shifts(low((place(4)[:16], place(4)[16:])), 0, 2)
    far = shifts(low((place(3), place(5))), 0)
    sums = add_halves(add_on((place(2), place(6)), far), farthest)
    near = shifts(low((place(1), place(7))), 0)
    middle = shifts(low(sums), 0, 2)
    return place(0) + sum(part.astype(F32) for part in near + middle)


def per_device(tokens, cotangent, segment_ids, w_qkv, w_out, m_qkv, v_qkv, m_out, v_out):
    own = jnp.concatenate([w_qkv[0].astype(BF16), to_rows(w_out[0].astype(BF16))], 1)
    widened = tokens[0].astype(F32)
    normed = (
        widened * lax.rsqrt(jnp.mean(widened * widened, -1, keepdims=True) + norm_eps)
    ).astype(BF16)

    def prepare(blocks):
        return (
            mixed_product("ld,de->le", normed, reorder_matrix(blocks, 32)).astype(BF16),
            reorder_matrix(blocks, 16),
        )

    (line_qkv, q1, q2, q3, q4), (line_out, *moved_out), own_late, (normed, reorder_heads) = gather_rows(
        own, prepare
    )
    beside = lax.ppermute(own_late, "blk", [(i, (i + 1) % 4) for i in range(4)])
    seg_row = segment_ids
    seg_col = segment_ids.reshape(LENGTH, 1)

    joined = 0.0
    for low_row, part in (
        (0, line_qkv), (256, q1[1]), (1792, q1[0]), (512, q2[1]), (1536, q2[0]),
        (768, q3[1]), (1280, q3[0]), (1024, q4[0]), (1152, q4[1]),
    ):
        features = normed[:, low_row : low_row + part.shape[0]]
        joined = joined + mixed_product("ld,de->le", features, part)
    joined = joined.astype(BF16)
    attended = on_core(
        forward_kernel, HQ, [pltpu.VMEM((LENGTH, HQ), BF16)], 1300000000,
        joined, seg_col, seg_row, reorder_heads,
    )
    moved_out, attended, beside = tie(moved_out, attended, beside)
    beside = beside.astype(F32)
    beside_qkv, beside_out = beside[:, :COLS][None], from_rows(beside[:, COLS:])[None]
    full_out = jnp.concatenate(by_offset(line_out, moved_out), 0)
    sum_out, joined_late = line_sum(
        lambda k, held: mixed_product("ld,le->de", held[:, 128 * k : 128 * (k + 1)], cotangent[0]),
        attended, joined,
    )
    grad_rel = mixed_product("ld,ed->le", cotangent[0], full_out).astype(BF16)
    grads = [
        on_core(
            functools.partial(backward_kernel, kv), (GROUP + 2) * HD,
            [pltpu.VMEM((LENGTH, GROUP * HD), BF16), pltpu.VMEM((LENGTH, 2 * HD), F32)], 1250000000,
            source, seg_col, seg_row, reorder_heads, grad_rel,
        )
        for kv, source in enumerate((joined, joined_late))
    ]
    wide = GROUP * HD
    joined_grad = jnp.concatenate(
        [
            *[part[:, :wide] for part in grads],
            *[part[:, wide : wide + HD] for part in grads],
            *[part[:, wide + HD :] for part in grads],
        ],
        1,
    )
    sum_qkv, _ = line_sum(
        lambda k, held: mixed_product("ld,le->de", normed[:, 256 * k : 256 * (k + 1)], held), joined_grad
    )
    layer_out = (
        tokens[0].astype(F32) + mixed_product("le,ed->ld", attended, full_out)
    ).astype(BF16)
    summed = small_sum(jnp.concatenate([sum_qkv, to_rows(sum_out)], 1))
    grad_qkv, grad_out = summed[:, :COLS], from_rows(summed[:, COLS:])

    new_qkv, new_m_qkv, new_v_qkv = adamw(w_qkv, m_qkv, v_qkv, grad_qkv[None], beside_qkv)
    new_out, new_m_out, new_v_out = adamw(w_out, m_out, v_out, grad_out[None], beside_out)
    return (layer_out[None], new_qkv, new_out, new_m_qkv, new_v_qkv, new_m_out, new_v_out)


def solution(mesh):
    rows, row = P("blk", "fsdp", None), P("blk", "fsdp")
    return jax.shard_map(
        per_device,
        mesh=mesh,
        in_specs=(rows, rows, row) + (rows,) * 6,
        out_specs=(rows,) * 7,
        check_vma=False,
    )
```

```python
import functools

import jax
import jax.numpy as jnp
from jax import lax
from jax.experimental import pallas as pl
from jax.experimental.pallas import tpu as pltpu
from jax.sharding import PartitionSpec as P

HEADS = 8
KV_HEADS = 2
HD = 128
HQ = 1024
KVW = 256
COLS = 1536
RING = 8
LENGTH = 384
BLOCK = 128
GROUP = HEADS // KV_HEADS

norm_eps = 1e-05
beta_one = 0.9
beta_two = 0.95
learn_rate = 0.01
decay_rate = 0.1
adam_eps = 1e-08
masked_score = -1e30

BOTH = ("blk", "fsdp")
F32 = jnp.float32
BF16 = jnp.bfloat16


def coords(device):
    block, index = divmod(device, 64)
    y, x, z = index // 16, index // 8 % 2, index % 8
    cycle = y if x == 0 else 7 - y
    return block, ((z, cycle) if block % 2 == 0 else (cycle, z))


def device_at(block, first, second):
    z, cycle = (first, second) if block % 2 == 0 else (second, first)
    y, x = (cycle, 0) if cycle < 4 else (7 - cycle, 1)
    return block * 64 + y * 16 + x * 8 + z


def ring_shift(value, ring, by):
    pairs = []
    for device in range(256):
        block, (first, second) = coords(device)
        if ring == 0:
            target = device_at(block, (first + by) % RING, second)
        else:
            target = device_at(block, first, (second + by) % RING)
        pairs.append((device, target))
    return lax.ppermute(value, BOTH, pairs)


def absolute_blocks():
    block, index = lax.axis_index("blk"), lax.axis_index("fsdp")
    even = block % 2 == 0
    y, x, z = index // 16, index // 8 % 2, index % 8
    cycle = jnp.where(x == 0, y, 7 - y)
    first, second = jnp.where(even, z, cycle), jnp.where(even, cycle, z)
    steps = jnp.arange(RING)
    first = jnp.broadcast_to(((first + steps) % RING)[None, :], (RING, RING))
    second = jnp.broadcast_to(((second + steps) % RING)[:, None], (RING, RING))
    z, cycle = jnp.where(even, first, second), jnp.where(even, second, first)
    y, x = jnp.where(cycle < 4, cycle, 7 - cycle), (cycle >= 4).astype(jnp.int32)
    return (y * 16 + x * 8 + z).reshape(64)


def reorder_matrix(blocks, rows):
    source = (blocks[:, None] * rows + jnp.arange(rows)[None, :]).reshape(-1)
    return (jnp.arange(64 * rows)[:, None] == source[None, :]).astype(BF16)


def shifts(pair, ring, places=1):
    return ring_shift(pair[0], ring, places), ring_shift(pair[1], ring, -places)


def halves(pair):
    half = pair[0].shape[0] // 2
    return pair[0][:half], pair[1][half:]


def tie(*trees):
    return lax.optimization_barrier(trees)


def by_offset(own, steps):
    one, two, three, four = steps
    return [own, one[1], two[1], three[1], jnp.concatenate(four, 0), three[0], two[0], one[0]]


def low(pair):
    return pair[0].astype(BF16), pair[1].astype(BF16)


def add_on(shares, pair):
    return shares[0] + pair[0].astype(F32), shares[1] + pair[1].astype(F32)


def add_halves(shares, pair):
    half = shares[0].shape[0] // 2
    up, down = pair[0].astype(F32), pair[1].astype(F32)
    return (
        jnp.concatenate([shares[0][:half] + up, shares[0][half:]], 0),
        jnp.concatenate([shares[1][:half], shares[1][half:] + down], 0),
    )


def mixed_product(formula, first_op, second_op):
    return jnp.einsum(formula, first_op, second_op, preferred_element_type=F32)


def block_probs(joined, seg_col, seg_row, kv, block):
    low, high = block * BLOCK, (block + 1) * BLOCK
    start = max(low - BLOCK, 0)
    queries = jnp.concatenate(
        [joined[low:high, HD * head : HD * (head + 1)] for head in range(GROUP * kv, GROUP * (kv + 1))], 0
    )
    keys = joined[start:high, HQ + HD * kv : HQ + HD * (kv + 1)]
    scores = lax.dot_general(
        queries, keys, (((1,), (1,)), ((), ())), preferred_element_type=F32
    ) * HD ** (-0.5)
    shape = (BLOCK, high - start)
    position = low + lax.broadcasted_iota(jnp.int32, shape, 0)
    other = start + lax.broadcasted_iota(jnp.int32, shape, 1)
    allowed = (seg_col[low:high, :] == seg_row[:, start:high]) & (position >= other)
    bias = jnp.where(allowed, 1, 0)
    scores = jnp.where(jnp.concatenate([bias] * GROUP, 0) > 0, scores, masked_score)
    raised = jnp.exp(scores - jnp.max(scores, -1, keepdims=True))
    return queries, keys, raised / jnp.sum(raised, -1, keepdims=True)


def forward_kernel(joined, seg_col, seg_row, reorder, attended, plain):
    for kv in range(KV_HEADS):
        for block in range(3):
            low, high = block * BLOCK, (block + 1) * BLOCK
            start = max(low - BLOCK, 0)
            _, _, probs = block_probs(joined, seg_col, seg_row, kv, block)
            values = joined[start:high, HQ + KVW + HD * kv : HQ + KVW + HD * (kv + 1)]
            found = jnp.dot(probs.astype(BF16), values, preferred_element_type=F32).astype(BF16)
            for head in range(GROUP):
                at = HD * (GROUP * kv + head)
                plain[low:high, at : at + HD] = found[BLOCK * head : BLOCK * (head + 1)]
    attended[...] = jnp.dot(plain[...], reorder[...], preferred_element_type=F32).astype(BF16)


def backward_kernel(kv, joined, seg_col, seg_row, reorder, grad_rel, grads, upstream, kv_sums):
    wide = GROUP * HD
    upstream[...] = lax.dot_general(
        grad_rel[...], reorder[wide * kv : wide * (kv + 1)], (((1,), (1,)), ((), ())), preferred_element_type=F32
    ).astype(BF16)
    across = (((0,), (0,)), ((), ()))
    kv_sums[...] = jnp.zeros_like(kv_sums)
    for block in range(3):
        low, high = block * BLOCK, (block + 1) * BLOCK
        start = max(low - BLOCK, 0)
        queries, keys, probs = block_probs(joined, seg_col, seg_row, kv, block)
        values = joined[start:high, HQ + KVW + HD * kv : HQ + KVW + HD * (kv + 1)]
        grad_att = jnp.concatenate(
            [upstream[low:high, HD * head : HD * (head + 1)] for head in range(GROUP)], 0
        )
        grad_probs = lax.dot_general(
            grad_att, values, (((1,), (1,)), ((), ())), preferred_element_type=F32
        )
        kv_sums[start:high, HD:] += lax.dot_general(
            probs.astype(BF16), grad_att, across, preferred_element_type=F32
        )
        centred = grad_probs - jnp.sum(grad_probs * probs, -1, keepdims=True)
        grad_scores = (probs * centred * HD ** (-0.5)).astype(BF16)
        found = jnp.dot(grad_scores, keys, preferred_element_type=F32).astype(BF16)
        for head in range(GROUP):
            grads[low:high, HD * head : HD * (head + 1)] = found[BLOCK * head : BLOCK * (head + 1)]
        kv_sums[start:high, :HD] += lax.dot_general(
            grad_scores, queries, across, preferred_element_type=F32
        )
    grads[:, wide:] = kv_sums[...].astype(BF16)


def on_core(kernel, width, scratch, flops, *operands):
    whole = pl.BlockSpec(memory_space=pltpu.VMEM)
    return pl.pallas_call(
        kernel,
        out_shape=jax.ShapeDtypeStruct((LENGTH, width), BF16),
        in_specs=[whole] * len(operands),
        out_specs=whole,
        scratch_shapes=scratch,
        compiler_params=pltpu.CompilerParams(vmem_limit_bytes=40 * 2**20),
        cost_estimate=pl.CostEstimate(flops=flops, bytes_accessed=6 * 2**20, transcendentals=2**20),
    )(*operands)


def adamw(weights, moment, second, gradient, beside):
    moment_new = beta_one * moment + (1.0 - beta_one) * gradient
    second_new = beta_two * second + (1.0 - beta_two) * gradient * gradient
    stepped = weights - learn_rate * (
        moment_new / (jnp.sqrt(second_new) + adam_eps) + decay_rate * weights
    )
    return (0.5 * (stepped + beside), moment_new, second_new)


def to_rows(out_rows):
    left = out_rows[:, :1024].reshape(-1, 16, 1024)
    right = out_rows[:, 1024:].reshape(-1, 16, 1024)
    return jnp.concatenate([left, right], 1).reshape(-1, 1024)


def from_rows(rows):
    split = rows.reshape(-1, 32, 1024)
    left, right = split[:, :16].reshape(-1, 1024), split[:, 16:].reshape(-1, 1024)
    return jnp.concatenate([left, right], 1)


def sort_kernel(*refs):
    *pieces, rows_qkv, rows_out = refs
    at = 0
    for piece in pieces:
        rows = piece.shape[0]
        rows_qkv[at : at + rows] = piece[:, :COLS]
        half = at % 32 // 16
        for part in range(rows // 16):
            low, side = at // 32 * 16, 1024 * (half + part)
            rows_out[low : low + 16, side : side + 1024] = piece[16 * part : 16 * (part + 1), COLS:]
        at += rows


def sort_pieces(*pieces):
    whole = pl.BlockSpec(memory_space=pltpu.VMEM)
    return pl.pallas_call(
        sort_kernel,
        out_shape=(
            jax.ShapeDtypeStruct((256, COLS), BF16),
            jax.ShapeDtypeStruct((128, 2048), BF16),
        ),
        in_specs=[whole] * len(pieces),
        out_specs=(whole, whole),
        compiler_params=pltpu.CompilerParams(vmem_limit_bytes=16 * 2**20),
    )(*pieces)


def gather_rows(own, prepare):
    s1 = shifts((own, own), 0)
    s2 = shifts(s1, 0)
    s3 = shifts(s2, 0)
    s4 = shifts(halves(s3), 0)
    line_qkv, line_out = sort_pieces(
        own, s1[1], s2[1], s3[1], s4[0], s4[1], s3[0], s2[0], s1[0]
    )
    line_qkv, line_out, blocks = tie(line_qkv, line_out, absolute_blocks())
    prepared = prepare(blocks)
    q1 = shifts((line_qkv, line_qkv), 1)
    q1, line_out, prepared = tie(q1, line_out, prepared)
    q2 = shifts(q1, 1)
    o1 = shifts((line_out, line_out), 1)
    q3 = shifts(q2, 1)
    o2 = shifts(o1, 1)
    q3, own = tie(q3, own)
    q4 = shifts(halves(q3), 1)
    o3 = shifts(o2, 1)
    o4 = shifts(halves(o3), 1)
    return (line_qkv, q1, q2, q3, q4), (line_out, o1, o2, o3, o4), own, prepared


def line_sum(share, waiting, after_first=None):
    farthest = share(4, waiting)
    half = farthest.shape[0] // 2
    beside = share(3, waiting), share(5, waiting)
    moved = shifts(low((farthest[:half], farthest[half:])), 1)
    moved, waiting, after_first = tie(moved, waiting, after_first)
    sums = add_halves(beside, moved)
    for step in (2, 1):
        beside = share(step, waiting), share(RING - step, waiting)
        moved = shifts(low(sums), 1)
        moved, waiting = tie(moved, waiting)
        sums = add_on(beside, moved)
    last = share(0, waiting)
    moved = shifts(low(sums), 1)
    return last + moved[0].astype(F32) + moved[1].astype(F32), after_first


def small_sum(rows):
    place = lambda k: rows[32 * k : 32 * (k + 1)]
    farthest = shifts(low((place(4)[:16], place(4)[16:])), 0, 2)
    far = shifts(low((place(3), place(5))), 0)
    sums = add_halves(add_on((place(2), place(6)), far), farthest)
    near = shifts(low((place(1), place(7))), 0)
    middle = shifts(low(sums), 0, 2)
    return place(0) + sum(part.astype(F32) for part in near + middle)


def per_device(tokens, cotangent, segment_ids, w_qkv, w_out, m_qkv, v_qkv, m_out, v_out):
    own = jnp.concatenate([w_qkv[0].astype(BF16), to_rows(w_out[0].astype(BF16))], 1)
    widened = tokens[0].astype(F32)
    normed = (
        widened * lax.rsqrt(jnp.mean(widened * widened, -1, keepdims=True) + norm_eps)
    ).astype(BF16)

    def prepare(blocks):
        return (
            mixed_product("ld,de->le", normed, reorder_matrix(blocks, 32)).astype(BF16),
            reorder_matrix(blocks, 16),
        )

    (line_qkv, q1, q2, q3, q4), (line_out, *moved_out), own_late, (normed, reorder_heads) = gather_rows(
        own, prepare
    )
    beside = lax.ppermute(own_late, "blk", [(i, (i + 1) % 4) for i in range(4)])
    seg_row = segment_ids
    seg_col = segment_ids.reshape(LENGTH, 1)

    joined = 0.0
    for low_row, part in (
        (0, line_qkv), (256, q1[1]), (1792, q1[0]), (512, q2[1]), (1536, q2[0]),
        (768, q3[1]), (1280, q3[0]), (1024, q4[0]), (1152, q4[1]),
    ):
        features = normed[:, low_row : low_row + part.shape[0]]
        joined = joined + mixed_product("ld,de->le", features, part)
    joined = joined.astype(BF16)
    attended = on_core(
        forward_kernel, HQ, [pltpu.VMEM((LENGTH, HQ), BF16)], 1300000000,
        joined, seg_col, seg_row, reorder_heads,
    )
    moved_out, attended, beside = tie(moved_out, attended, beside)
    beside = beside.astype(F32)
    beside_qkv, beside_out = beside[:, :COLS][None], from_rows(beside[:, COLS:])[None]
    full_out = jnp.concatenate(by_offset(line_out, moved_out), 0)
    sum_out, joined_late = line_sum(
        lambda k, held: mixed_product("ld,le->de", held[:, 128 * k : 128 * (k + 1)], cotangent[0]),
        attended, joined,
    )
    grad_rel = mixed_product("ld,ed->le", cotangent[0], full_out).astype(BF16)
    grads = [
        on_core(
            functools.partial(backward_kernel, kv), (GROUP + 2) * HD,
            [pltpu.VMEM((LENGTH, GROUP * HD), BF16), pltpu.VMEM((LENGTH, 2 * HD), F32)], 1250000000,
            source, seg_col, seg_row, reorder_heads, grad_rel,
        )
        for kv, source in enumerate((joined, joined_late))
    ]
    wide = GROUP * HD
    joined_grad = jnp.concatenate(
        [
            *[part[:, :wide] for part in grads],
            *[part[:, wide : wide + HD] for part in grads],
            *[part[:, wide + HD :] for part in grads],
        ],
        1,
    )
    sum_qkv, _ = line_sum(
        lambda k, held: mixed_product("ld,le->de", normed[:, 256 * k : 256 * (k + 1)], held), joined_grad
    )
    sum_out, attended = tie(sum_out, attended)
    layer_out = (
        tokens[0].astype(F32) + mixed_product("le,ed->ld", attended, full_out)
    ).astype(BF16)
    summed = small_sum(jnp.concatenate([sum_qkv, to_rows(sum_out)], 1))
    grad_qkv, grad_out = summed[:, :COLS], from_rows(summed[:, COLS:])

    new_qkv, new_m_qkv, new_v_qkv = adamw(w_qkv, m_qkv, v_qkv, grad_qkv[None], beside_qkv)
    new_out, new_m_out, new_v_out = adamw(w_out, m_out, v_out, grad_out[None], beside_out)
    return (layer_out[None], new_qkv, new_out, new_m_qkv, new_v_qkv, new_m_out, new_v_out)


def solution(mesh):
    rows, row = P("blk", "fsdp", None), P("blk", "fsdp")
    return jax.shard_map(
        per_device,
        mesh=mesh,
        in_specs=(rows, rows, row) + (rows,) * 6,
        out_specs=(rows,) * 7,
        check_vma=False,
    )
```

```python
import functools

import jax
import jax.numpy as jnp
from jax import lax
from jax.experimental import pallas as pl
from jax.experimental.pallas import tpu as pltpu
from jax.sharding import PartitionSpec as P

HEADS = 8
KV_HEADS = 2
HD = 128
HQ = 1024
KVW = 256
COLS = 1536
RING = 8
LENGTH = 384
BLOCK = 128
GROUP = HEADS // KV_HEADS

norm_eps = 1e-05
beta_one = 0.9
beta_two = 0.95
learn_rate = 0.01
decay_rate = 0.1
adam_eps = 1e-08
masked_score = -1e30

BOTH = ("blk", "fsdp")
F32 = jnp.float32
BF16 = jnp.bfloat16


def coords(device):
    block, index = divmod(device, 64)
    y, x, z = index // 16, index // 8 % 2, index % 8
    cycle = y if x == 0 else 7 - y
    return block, ((z, cycle) if block % 2 == 0 else (cycle, z))


def device_at(block, first, second):
    z, cycle = (first, second) if block % 2 == 0 else (second, first)
    y, x = (cycle, 0) if cycle < 4 else (7 - cycle, 1)
    return block * 64 + y * 16 + x * 8 + z


def ring_shift(value, ring, by):
    pairs = []
    for device in range(256):
        block, (first, second) = coords(device)
        if ring == 0:
            target = device_at(block, (first + by) % RING, second)
        else:
            target = device_at(block, first, (second + by) % RING)
        pairs.append((device, target))
    return lax.ppermute(value, BOTH, pairs)


def absolute_blocks():
    block, index = lax.axis_index("blk"), lax.axis_index("fsdp")
    even = block % 2 == 0
    y, x, z = index // 16, index // 8 % 2, index % 8
    cycle = jnp.where(x == 0, y, 7 - y)
    first, second = jnp.where(even, z, cycle), jnp.where(even, cycle, z)
    steps = jnp.arange(RING)
    first = jnp.broadcast_to(((first + steps) % RING)[None, :], (RING, RING))
    second = jnp.broadcast_to(((second + steps) % RING)[:, None], (RING, RING))
    z, cycle = jnp.where(even, first, second), jnp.where(even, second, first)
    y, x = jnp.where(cycle < 4, cycle, 7 - cycle), (cycle >= 4).astype(jnp.int32)
    return (y * 16 + x * 8 + z).reshape(64)


def reorder_matrix(blocks, rows):
    source = (blocks[:, None] * rows + jnp.arange(rows)[None, :]).reshape(-1)
    return (jnp.arange(64 * rows)[:, None] == source[None, :]).astype(BF16)


def shifts(pair, ring, places=1):
    return ring_shift(pair[0], ring, places), ring_shift(pair[1], ring, -places)


def halves(pair):
    half = pair[0].shape[0] // 2
    return pair[0][:half], pair[1][half:]


def tie(*trees):
    return lax.optimization_barrier(trees)


def by_offset(own, steps):
    one, two, three, four = steps
    return [own, one[1], two[1], three[1], jnp.concatenate(four, 0), three[0], two[0], one[0]]


def low(pair):
    return pair[0].astype(BF16), pair[1].astype(BF16)


def add_on(shares, pair):
    return shares[0] + pair[0].astype(F32), shares[1] + pair[1].astype(F32)


def add_halves(shares, pair):
    half = shares[0].shape[0] // 2
    up, down = pair[0].astype(F32), pair[1].astype(F32)
    return (
        jnp.concatenate([shares[0][:half] + up, shares[0][half:]], 0),
        jnp.concatenate([shares[1][:half], shares[1][half:] + down], 0),
    )


def mixed_product(formula, first_op, second_op):
    return jnp.einsum(formula, first_op, second_op, preferred_element_type=F32)


def block_probs(joined, seg_col, seg_row, kv, block):
    low, high = block * BLOCK, (block + 1) * BLOCK
    start = max(low - BLOCK, 0)
    queries = jnp.concatenate(
        [joined[low:high, HD * head : HD * (head + 1)] for head in range(GROUP * kv, GROUP * (kv + 1))], 0
    )
    keys = joined[start:high, HQ + HD * kv : HQ + HD * (kv + 1)]
    scores = lax.dot_general(
        queries, keys, (((1,), (1,)), ((), ())), preferred_element_type=F32
    ) * HD ** (-0.5)
    shape = (BLOCK, high - start)
    position = low + lax.broadcasted_iota(jnp.int32, shape, 0)
    other = start + lax.broadcasted_iota(jnp.int32, shape, 1)
    allowed = (seg_col[low:high, :] == seg_row[:, start:high]) & (position >= other)
    bias = jnp.where(allowed, 1, 0)
    scores = jnp.where(jnp.concatenate([bias] * GROUP, 0) > 0, scores, masked_score)
    raised = jnp.exp(scores - jnp.max(scores, -1, keepdims=True))
    return queries, keys, raised / jnp.sum(raised, -1, keepdims=True)


def forward_kernel(joined, seg_col, seg_row, reorder, attended, plain):
    for kv in range(KV_HEADS):
        for block in range(3):
            low, high = block * BLOCK, (block + 1) * BLOCK
            start = max(low - BLOCK, 0)
            _, _, probs = block_probs(joined, seg_col, seg_row, kv, block)
            values = joined[start:high, HQ + KVW + HD * kv : HQ + KVW + HD * (kv + 1)]
            found = jnp.dot(probs.astype(BF16), values, preferred_element_type=F32).astype(BF16)
            for head in range(GROUP):
                at = HD * (GROUP * kv + head)
                plain[low:high, at : at + HD] = found[BLOCK * head : BLOCK * (head + 1)]
    attended[...] = jnp.dot(plain[...], reorder[...], preferred_element_type=F32).astype(BF16)


def backward_kernel(kv, joined, seg_col, seg_row, reorder, grad_rel, grads, upstream, kv_sums):
    wide = GROUP * HD
    upstream[...] = lax.dot_general(
        grad_rel[...], reorder[wide * kv : wide * (kv + 1)], (((1,), (1,)), ((), ())), preferred_element_type=F32
    ).astype(BF16)
    across = (((0,), (0,)), ((), ()))
    kv_sums[...] = jnp.zeros_like(kv_sums)
    for block in range(3):
        low, high = block * BLOCK, (block + 1) * BLOCK
        start = max(low - BLOCK, 0)
        queries, keys, probs = block_probs(joined, seg_col, seg_row, kv, block)
        values = joined[start:high, HQ + KVW + HD * kv : HQ + KVW + HD * (kv + 1)]
        grad_att = jnp.concatenate(
            [upstream[low:high, HD * head : HD * (head + 1)] for head in range(GROUP)], 0
        )
        grad_probs = lax.dot_general(
            grad_att, values, (((1,), (1,)), ((), ())), preferred_element_type=F32
        )
        kv_sums[start:high, HD:] += lax.dot_general(
            probs.astype(BF16), grad_att, across, preferred_element_type=F32
        )
        centred = grad_probs - jnp.sum(grad_probs * probs, -1, keepdims=True)
        grad_scores = (probs * centred * HD ** (-0.5)).astype(BF16)
        found = jnp.dot(grad_scores, keys, preferred_element_type=F32).astype(BF16)
        for head in range(GROUP):
            grads[low:high, HD * head : HD * (head + 1)] = found[BLOCK * head : BLOCK * (head + 1)]
        kv_sums[start:high, :HD] += lax.dot_general(
            grad_scores, queries, across, preferred_element_type=F32
        )
    grads[:, wide:] = kv_sums[...].astype(BF16)


def on_core(kernel, width, scratch, flops, *operands):
    whole = pl.BlockSpec(memory_space=pltpu.VMEM)
    return pl.pallas_call(
        kernel,
        out_shape=jax.ShapeDtypeStruct((LENGTH, width), BF16),
        in_specs=[whole] * len(operands),
        out_specs=whole,
        scratch_shapes=scratch,
        compiler_params=pltpu.CompilerParams(vmem_limit_bytes=40 * 2**20),
        cost_estimate=pl.CostEstimate(flops=flops, bytes_accessed=6 * 2**20, transcendentals=2**20),
    )(*operands)


def adamw(weights, moment, second, gradient, beside):
    moment_new = beta_one * moment + (1.0 - beta_one) * gradient
    second_new = beta_two * second + (1.0 - beta_two) * gradient * gradient
    stepped = weights - learn_rate * (
        moment_new / (jnp.sqrt(second_new) + adam_eps) + decay_rate * weights
    )
    return (0.5 * (stepped + beside), moment_new, second_new)


def to_rows(out_rows):
    left = out_rows[:, :1024].reshape(-1, 16, 1024)
    right = out_rows[:, 1024:].reshape(-1, 16, 1024)
    return jnp.concatenate([left, right], 1).reshape(-1, 1024)


def from_rows(rows):
    split = rows.reshape(-1, 32, 1024)
    left, right = split[:, :16].reshape(-1, 1024), split[:, 16:].reshape(-1, 1024)
    return jnp.concatenate([left, right], 1)


def sort_kernel(*refs):
    *pieces, rows_qkv, rows_out = refs
    at = 0
    for piece in pieces:
        rows = piece.shape[0]
        rows_qkv[at : at + rows] = piece[:, :COLS]
        half = at % 32 // 16
        for part in range(rows // 16):
            low, side = at // 32 * 16, 1024 * (half + part)
            rows_out[low : low + 16, side : side + 1024] = piece[16 * part : 16 * (part + 1), COLS:]
        at += rows


def sort_pieces(*pieces):
    whole = pl.BlockSpec(memory_space=pltpu.VMEM)
    return pl.pallas_call(
        sort_kernel,
        out_shape=(
            jax.ShapeDtypeStruct((256, COLS), BF16),
            jax.ShapeDtypeStruct((128, 2048), BF16),
        ),
        in_specs=[whole] * len(pieces),
        out_specs=(whole, whole),
        compiler_params=pltpu.CompilerParams(vmem_limit_bytes=16 * 2**20),
    )(*pieces)


def gather_rows(own, prepare):
    s1 = shifts((own, own), 0)
    s2 = shifts(s1, 0)
    s3 = shifts(s2, 0)
    s4 = shifts(halves(s3), 0)
    line_qkv, line_out = sort_pieces(
        own, s1[1], s2[1], s3[1], s4[0], s4[1], s3[0], s2[0], s1[0]
    )
    line_qkv, line_out, blocks = tie(line_qkv, line_out, absolute_blocks())
    prepared = prepare(blocks)
    q1 = shifts((line_qkv, line_qkv), 1)
    q1, line_out, prepared = tie(q1, line_out, prepared)
    q2 = shifts(q1, 1)
    o1 = shifts((line_out, line_out), 1)
    q3 = shifts(q2, 1)
    o2 = shifts(o1, 1)
    q3, own = tie(q3, own)
    q4 = shifts(halves(q3), 1)
    o3 = shifts(o2, 1)
    o4 = shifts(halves(o3), 1)
    return (line_qkv, q1, q2, q3, q4), (line_out, o1, o2, o3, o4), own, prepared


def line_sum(share, waiting, after_first=None):
    farthest = share(4, waiting)
    half = farthest.shape[0] // 2
    beside = share(3, waiting), share(5, waiting)
    moved = shifts(low((farthest[:half], farthest[half:])), 1)
    moved, waiting, after_first = tie(moved, waiting, after_first)
    sums = add_halves(beside, moved)
    for step in (2, 1):
        beside = share(step, waiting), share(RING - step, waiting)
        moved = shifts(low(sums), 1)
        moved, waiting = tie(moved, waiting)
        sums = add_on(beside, moved)
    last = share(0, waiting)
    moved = shifts(low(sums), 1)
    return last + moved[0].astype(F32) + moved[1].astype(F32), after_first


def small_sum(rows):
    place = lambda k: rows[32 * k : 32 * (k + 1)]
    farthest = shifts(low((place(4)[:16], place(4)[16:])), 0, 2)
    far = shifts(low((place(3), place(5))), 0)
    sums = add_halves(add_on((place(2), place(6)), far), farthest)
    near = shifts(low((place(1), place(7))), 0)
    middle = shifts(low(sums), 0, 2)
    return place(0) + sum(part.astype(F32) for part in near + middle)


def per_device(tokens, cotangent, segment_ids, w_qkv, w_out, m_qkv, v_qkv, m_out, v_out):
    own = jnp.concatenate([w_qkv[0].astype(BF16), to_rows(w_out[0].astype(BF16))], 1)
    widened = tokens[0].astype(F32)
    normed = (
        widened * lax.rsqrt(jnp.mean(widened * widened, -1, keepdims=True) + norm_eps)
    ).astype(BF16)

    def prepare(blocks):
        return (
            mixed_product("ld,de->le", normed, reorder_matrix(blocks, 32)).astype(BF16),
            reorder_matrix(blocks, 16),
        )

    (line_qkv, q1, q2, q3, q4), (line_out, *moved_out), own_late, (normed, reorder_heads) = gather_rows(
        own, prepare
    )
    beside = lax.ppermute(own_late, "blk", [(i, (i + 1) % 4) for i in range(4)])
    seg_row = segment_ids
    seg_col = segment_ids.reshape(LENGTH, 1)

    joined = 0.0
    for low_row, part in (
        (0, line_qkv), (256, q1[1]), (1792, q1[0]), (512, q2[1]), (1536, q2[0]),
        (768, q3[1]), (1280, q3[0]), (1024, q4[0]), (1152, q4[1]),
    ):
        features = normed[:, low_row : low_row + part.shape[0]]
        joined = joined + mixed_product("ld,de->le", features, part)
    joined = joined.astype(BF16)
    attended = on_core(
        forward_kernel, HQ, [pltpu.VMEM((LENGTH, HQ), BF16)], 1300000000,
        joined, seg_col, seg_row, reorder_heads,
    )
    moved_out, attended, beside = tie(moved_out, attended, beside)
    beside = beside.astype(F32)
    beside_qkv, beside_out = beside[:, :COLS][None], from_rows(beside[:, COLS:])[None]
    full_out = jnp.concatenate(by_offset(line_out, moved_out), 0)
    sum_out, joined_late = line_sum(
        lambda k, held: mixed_product("ld,le->de", held[:, 128 * k : 128 * (k + 1)], cotangent[0]),
        attended, joined,
    )
    grad_rel = mixed_product("ld,ed->le", cotangent[0], full_out).astype(BF16)
    grads = [
        on_core(
            functools.partial(backward_kernel, kv), (GROUP + 2) * HD,
            [pltpu.VMEM((LENGTH, GROUP * HD), BF16), pltpu.VMEM((LENGTH, 2 * HD), F32)], 1250000000,
            source, seg_col, seg_row, reorder_heads, grad_rel,
        )
        for kv, source in enumerate((joined, joined_late))
    ]
    wide = GROUP * HD
    joined_grad = jnp.concatenate(
        [
            *[part[:, :wide] for part in grads],
            *[part[:, wide : wide + HD] for part in grads],
            *[part[:, wide + HD :] for part in grads],
        ],
        1,
    )
    sum_qkv, _ = line_sum(
        lambda k, held: mixed_product("ld,le->de", normed[:, 256 * k : 256 * (k + 1)], held), joined_grad
    )
    sum_qkv, attended = tie(sum_qkv, attended)
    layer_out = (
        tokens[0].astype(F32) + mixed_product("le,ed->ld", attended, full_out)
    ).astype(BF16)
    summed = small_sum(jnp.concatenate([sum_qkv, to_rows(sum_out)], 1))
    grad_qkv, grad_out = summed[:, :COLS], from_rows(summed[:, COLS:])

    new_qkv, new_m_qkv, new_v_qkv = adamw(w_qkv, m_qkv, v_qkv, grad_qkv[None], beside_qkv)
    new_out, new_m_out, new_v_out = adamw(w_out, m_out, v_out, grad_out[None], beside_out)
    return (layer_out[None], new_qkv, new_out, new_m_qkv, new_v_qkv, new_m_out, new_v_out)


def solution(mesh):
    rows, row = P("blk", "fsdp", None), P("blk", "fsdp")
    return jax.shard_map(
        per_device,
        mesh=mesh,
        in_specs=(rows, rows, row) + (rows,) * 6,
        out_specs=(rows,) * 7,
        check_vma=False,
    )
```
